32 devices in a mesh: clus: 8 (over z, y), rhs: 4 (over x, core).
Axes of the slice: x: 2, y: 2, z: 4, core: 2. Of those that a mesh axis runs over, the one named last changes fastest.
Arguments:
- rhs_in: bfloat16 [2, 32, 4096], P(None, 'rhs', 'clus'), may hold values from -6 to 6
- row_basis: bfloat16 [16, 2, 96, 256], P('clus'), may hold values from -0.25 to 0.25
- col_basis: bfloat16 [16, 2, 96, 256], P('clus'), may hold values from -0.09375 to 0.09375
- coupling: bfloat16 [16, 24, 96, 192], P('clus', 'rhs'), may hold values from -0.4375 to 0.4375
- far_col: int32 [16, 24], P('clus', 'rhs'), may hold values from 0 to 15, as said below
- cluster_rank: int32 [16], P('clus'), may hold values from 32 to 96
- near_block: bfloat16 [16, 16, 2, 256, 256], P('clus', 'rhs'), may hold values from -0.0625 to 0.0625
- near_col: int32 [16, 16], P('clus', 'rhs'), may hold values from 0 to 15, as said below
Outputs:
- adjoint_out: bfloat16 [2, 32, 4096], P(None, 'rhs', 'clus')
The draws below stay inside these ranges and needn't reach their ends.
Inputs may be any that keep to these rules, and one draw needn't show every extreme that they name: `near_col`: each entry lies within 2 clusters of its own row cluster; slot 0 is the row cluster itself and slot 1 lies exactly 2 clusters away from it. `far_col`: of the far blocks held by one device (rows of 2 row clusters, 24 / 4 blocks each), at most 2 have column clusters in the same aligned group of 2 clusters c * 2 to (c + 1) * 2 - 1, and some group receives exactly 2.
All inputs are finite; a program needn't handle non-finite values.
Results may differ from the reference program's by a relative error of at most 0.0044.
Values may be sent and summed in bfloat16 or wider, within the bound.
A program may use at most 64 MiB of HBM per device.

```python
import jax
import jax.numpy as jnp
from jax import lax

M = 256
K = 96
R = 32
NB = 16
FB = 24
CL_DEV = 2
NC = 16
COEFFS = 4096
N_CLUS = 8
N_RHS = 4


def draw_near_col(key, part):
    key = jax.random.fold_in(key, 7)
    row_ids = jnp.arange(NC, dtype=jnp.int32)[:, None]
    offsets = jax.random.randint(key, (NC, NB), -CL_DEV, CL_DEV + 1, dtype=jnp.int32)
    columns = jnp.clip(row_ids + offsets, 0, NC - 1)
    own_row = row_ids[:, 0]
    edge_col = jnp.where(own_row + CL_DEV < NC, own_row + CL_DEV, own_row - CL_DEV)
    columns = columns.at[:, 0].set(own_row)
    columns = columns.at[:, 1].set(edge_col)
    return columns.astype(jnp.int32)


def draw_far_col(key, part):
    key = jax.random.fold_in(key, 11)
    shift_key, member_key = jax.random.split(key)
    block_width = FB // N_RHS
    row_ids = jnp.arange(NC, dtype=jnp.int32)[:, None]
    slot_ids = jnp.arange(FB, dtype=jnp.int32)[None, :]
    owner = row_ids // CL_DEV
    within = row_ids % CL_DEV
    group = slot_ids // block_width
    local_block = within * block_width + slot_ids % block_width
    shifts = jax.random.randint(shift_key, (N_CLUS, N_RHS), 0, N_CLUS, dtype=jnp.int32)
    target = (shifts[owner, group] + local_block) % N_CLUS
    member = jax.random.randint(member_key, (NC, FB), 0, CL_DEV, dtype=jnp.int32)
    return (target * CL_DEV + member).astype(jnp.int32)


def set_ends(values, stream_key, low, top_value):
    longest = values.shape.index(max(values.shape))
    spots = []
    for shift in (0, 1):
        where = [jax.random.randint(jax.random.fold_in(stream_key, axis), (), 0, length) for axis, length in enumerate(values.shape)]
        where[longest] = (where[longest] + shift) % values.shape[longest]
        spots.append(tuple(where))
    return values.at[spots[0]].set(low).at[spots[1]].set(top_value)


def block_levels(own_key, extent, cuts, smallest, top_value):
    gain, own = 1.0, jax.random.fold_in(own_key, 6)
    for dim, blocks in cuts:
        heights = jnp.exp(jax.random.uniform(jax.random.fold_in(own, dim), (blocks,), jnp.float32, smallest / len(cuts), top_value / len(cuts)))
        gain = gain * jnp.repeat(heights, extent[dim] // blocks).reshape([-1 if axis == dim else 1 for axis in range(len(extent))])
    return gain


def bell_draw(rng, dims, deviation, limit, cuts=(), kind=jnp.bfloat16):
    level = block_levels(rng, dims, cuts, -0.22, 0.18) if cuts else 1.0
    array = jax.random.normal(rng, dims, jnp.float32) * deviation * level
    return jnp.minimum(jnp.maximum(array, -limit), limit).astype(kind)


def setup_inputs(seed: int = 0) -> dict:
    arg_keys = jax.random.split(jax.random.key(seed), 9)
    rhs_in = bell_draw(arg_keys[0], (2, R, COEFFS), 1.0, 6.0, ((1, 4), (2, 8)))
    row_basis = bell_draw(arg_keys[1], (NC, 2, K, M), (2 * M) ** -0.5, 0.25, ((0, 8),))
    col_basis = bell_draw(arg_keys[2], (NC, 2, K, M), (2 * K * FB) ** -0.5, 0.09375, ((0, 8),))
    coupling = bell_draw(arg_keys[3], (NC, FB, K, 2 * K), (2 * K) ** -0.5, 0.4375, ((0, 8), (1, 4)))
    far_col = draw_far_col(jax.random.fold_in(arg_keys[8], 71), 0)
    cluster_rank = set_ends(jax.random.randint(arg_keys[5], (NC,), K // 3, K + 1), jax.random.fold_in(arg_keys[5], 1), K // 3, K).astype(jnp.int32)
    near_block = bell_draw(arg_keys[6], (NC, NB, 2, M, M), (2 * M * NB) ** -0.5, 0.0625, ((0, 8), (1, 4)))
    near_col = draw_near_col(jax.random.fold_in(arg_keys[8], 71), 0)
    return {"rhs_in": rhs_in, "row_basis": row_basis, "col_basis": col_basis, "coupling": coupling, "far_col": far_col, "cluster_rank": cluster_rank, "near_block": near_block, "near_col": near_col}


def reference(rhs_in, row_basis, col_basis, coupling, far_col, cluster_rank, near_block, near_col):
    field_rows = rhs_in.astype(jnp.float32).reshape(2, R, NC, M).transpose(2, 0, 1, 3)
    rank_keep = (jnp.arange(K)[None, :] < cluster_rank[:, None]).astype(jnp.float32)
    projected = jnp.einsum("cprm,cqkm->cpqrk", field_rows, row_basis.astype(jnp.float32))
    coeff_re = projected[:, 0, 0] - projected[:, 1, 1]
    coeff_im = projected[:, 0, 1] + projected[:, 1, 0]
    basis_coeff = (jnp.stack([coeff_re, coeff_im], axis=1) * rank_keep[:, None, None, :]).astype(jnp.bfloat16)
    coupled = jnp.einsum("cprk,cfkl->cfprl", basis_coeff.astype(jnp.float32), coupling.astype(jnp.float32))
    term_re = coupled[:, :, 0, :, :K] - coupled[:, :, 1, :, K:]
    term_im = coupled[:, :, 0, :, K:] + coupled[:, :, 1, :, :K]
    far_term = jnp.stack([term_re, term_im], axis=2).reshape(NC * FB, 2, R, K)
    far_sum = jnp.zeros((NC, 2, R, K), jnp.float32).at[far_col.reshape(-1).astype(jnp.int32)].add(far_term)
    far_coeff = (far_sum * rank_keep[:, None, None, :]).astype(jnp.bfloat16)
    far_proj = jnp.einsum("cprk,cqkm->cpqrm", far_coeff.astype(jnp.float32), col_basis.astype(jnp.float32))
    far_field = jnp.stack([far_proj[:, 0, 0] - far_proj[:, 1, 1], far_proj[:, 0, 1] + far_proj[:, 1, 0]], axis=1)

    def near_step(accum_sum, inputs):
        rows_here, blocks_here, cols_here = inputs
        near_proj = jnp.einsum("prm,nqml->npqrl", rows_here, blocks_here.astype(jnp.float32))
        contrib = jnp.stack([near_proj[:, 0, 0] - near_proj[:, 1, 1], near_proj[:, 0, 1] + near_proj[:, 1, 0]], axis=1)
        return accum_sum.at[cols_here.astype(jnp.int32)].add(contrib), None

    near_field, _ = lax.scan(near_step, jnp.zeros((NC, 2, R, M), jnp.float32), (field_rows, near_block, near_col))
    combined = far_field + near_field
    return combined.transpose(1, 2, 0, 3).reshape(2, R, COEFFS).astype(jnp.bfloat16)
```

```python
import functools

import jax
import jax.numpy as jnp
from jax import lax
from jax.experimental import pallas as pl
from jax.experimental.pallas import tpu as pltpu
from jax.sharding import PartitionSpec as P

MESH = pl.DeviceIdType.MESH
F32 = jnp.float32
BF16 = jnp.bfloat16


def turned(v, half):
    parts = []
    for start in range(0, v.shape[0], 2 * half):
        parts.append(-v[start + half : start + 2 * half])
        parts.append(v[start : start + half])
    return jnp.concatenate(parts, axis=0)


def kernel(
    clus_n, rhs_n,
    rank_ref, fcol_ref, ncol_ref, x_ref, rb_hbm, cp_hbm, nb_hbm, cb_hbm,
    out_ref,
    rb, cp, nb, cb, xs, xr, terms, fsend, frecv, fown, fbs, fbr, prods, nsend, nrecv, nbs, nbr,
    load_sem, xs_sem, xr_sem, fs_sem, fr_sem, ns_sem, nr_sem, bs_sem, br_sem, ls_sem, lr_sem,
):
    me_c, me_r = lax.axis_index("clus"), lax.axis_index("rhs")
    half, leaf = x_ref.shape[1], nb.shape[3]
    rows = 2 * half
    local_n, near_n = nb.shape[0], nb.shape[1]
    far_n, rank_w = cp.shape[1], cp.shape[2]

    loads = [
        pltpu.make_async_copy(src, dst, load_sem.at[i])
        for i, (src, dst) in enumerate(((rb_hbm, rb), (cp_hbm, cp), (nb_hbm, nb), (cb_hbm, cb)))
    ]
    for load in loads:
        load.start()

    barrier = pltpu.get_barrier_semaphore()
    peers = [lax.rem(me_r + rhs_n - o, rhs_n) for o in range(rhs_n)]
    for o in range(1, rhs_n):
        pl.semaphore_signal(barrier, inc=1, device_id={"rhs": peers[o]}, device_id_type=MESH)

    def greet(o, carry):
        other = lax.rem(me_c + o, clus_n)
        pl.semaphore_signal(barrier, inc=1, device_id={"clus": other}, device_id_type=MESH)
        return carry

    lax.fori_loop(1, clus_n, greet, 0)
    xs[...] = jnp.concatenate([x_ref[0].astype(F32), x_ref[1].astype(F32)], axis=0).astype(BF16)

    @pl.when(me_c == 0)
    def _():
        nbr[0] = jnp.zeros_like(nbr[0])

    @pl.when(me_c == clus_n - 1)
    def _():
        nbr[1] = jnp.zeros_like(nbr[1])

    pl.semaphore_wait(barrier, rhs_n - 1 + clus_n - 1)

    def to_peer(src, dst, send, recv, o, forward=False):
        return pltpu.make_async_remote_copy(
            src_ref=src, dst_ref=dst.at[o - 1], send_sem=send.at[o - 1], recv_sem=recv.at[o - 1],
            device_id={"rhs": lax.rem(me_r + o, rhs_n) if forward else peers[o]}, device_id_type=MESH,
        )

    x_copies = [to_peer(xs, xr, xs_sem, xr_sem, o, forward=True) for o in range(1, rhs_n)]
    for copy in x_copies:
        copy.start()
    loads[0].wait()
    loads[1].wait()
    for copy in x_copies:
        copy.wait()

    fields = []
    for c in range(local_n):
        cols = slice(c * leaf, (c + 1) * leaf)
        plain = jnp.concatenate([xs[:, cols]] + [xr[o, :, cols] for o in range(rhs_n - 1)], axis=0)
        fields.append((plain, turned(plain.astype(F32), half).astype(BF16)))

    lanes = lax.broadcasted_iota(jnp.int32, (rhs_n * rows, rank_w), 1)
    last = (((1,), (1,)), ((), ()))
    for c in range(local_n):
        coeff = lax.dot_general(
            fields[c][0], rb[c, :rank_w], last, preferred_element_type=F32
        ) + lax.dot_general(fields[c][1], rb[c, rank_w:], last, preferred_element_type=F32)
        coeff = jnp.where(lanes < rank_ref[c], coeff, 0.0).astype(BF16)
        for f in range(far_n):
            coupled = jnp.dot(coeff, cp[c, f], preferred_element_type=F32)
            terms[c * far_n + f] = coupled[:, :rank_w] + turned(coupled[:, rank_w:], half)

    def spread(g, carry):
        for l in range(local_n):
            total = None
            for b in range(local_n * far_n):
                here = fcol_ref[b // far_n, b % far_n] == g * local_n + l
                part = terms[b] * jnp.where(here, 1.0, 0.0)
                total = part if total is None else total + part
            for o in range(rhs_n):
                fsend[o, g, l] = total[o * rows : (o + 1) * rows].astype(BF16)
        return carry

    lax.fori_loop(0, clus_n, spread, 0)
    f_copies = [to_peer(fsend.at[o], frecv, fs_sem, fr_sem, o) for o in range(1, rhs_n)]
    for copy in f_copies:
        copy.start()

    loads[2].wait()
    for c in range(local_n):
        both = jnp.concatenate(fields[c], axis=1)
        for n in range(near_n):
            prods[c * near_n + n] = jnp.dot(both, nb[c, n], preferred_element_type=F32)
    for d in range(3):
        for l in range(local_n):
            place = (d - 1) * local_n + l
            total = None
            for c in range(local_n):
                if abs(place - c) > 2:
                    continue
                for n in range(near_n):
                    here = ncol_ref[c, n] - me_c * local_n == place
                    part = prods[c * near_n + n] * jnp.where(here, 1.0, 0.0)
                    total = part if total is None else total + part
            for o in range(rhs_n):
                nsend[o, d, l] = total[o * rows : (o + 1) * rows].astype(BF16)
    n_copies = [to_peer(nsend.at[o], nrecv, ns_sem, nr_sem, o) for o in range(1, rhs_n)]
    for copy in n_copies:
        copy.start()

    for copy in f_copies:
        copy.wait_recv()

    def far_here(g):
        total = fsend[0, g].astype(F32)
        for o in range(rhs_n - 1):
            total += frecv[o, g].astype(F32)
        return total

    def far_copy(o):
        return pltpu.make_async_remote_copy(
            src_ref=fbs.at[o - 1], dst_ref=fbr.at[o - 1],
            send_sem=bs_sem.at[o - 1], recv_sem=br_sem.at[o - 1],
            device_id={"clus": lax.rem(me_c + o, clus_n)}, device_id_type=MESH,
        )

    def far_out(o, carry):
        fbs[o - 1] = far_here(lax.rem(me_c + o, clus_n)).astype(BF16)
        far_copy(o).start()
        return carry

    lax.fori_loop(1, clus_n, far_out, 0)
    fown[...] = far_here(me_c)

    for copy in n_copies:
        copy.wait_recv()

    def near_here(d):
        total = nsend[0, d].astype(F32)
        for o in range(rhs_n - 1):
            total += nrecv[o, d].astype(F32)
        return total

    def near_copy(side):
        other = me_c - 1 if side == 0 else me_c + 1
        return pltpu.make_async_remote_copy(
            src_ref=nbs.at[side], dst_ref=nbr.at[1 - side],
            send_sem=ls_sem.at[side], recv_sem=lr_sem.at[1 - side],
            device_id={"clus": other}, device_id_type=MESH,
        )

    nbs[0] = near_here(0).astype(BF16)

    @pl.when(me_c > 0)
    def _():
        near_copy(0).start()

    nbs[1] = near_here(2).astype(BF16)

    @pl.when(me_c < clus_n - 1)
    def _():
        near_copy(1).start()

    near_own = near_here(1)
    loads[3].wait()

    def far_in(o, total):
        far_copy(o).wait_recv()
        return total + fbr[o - 1].astype(F32)

    far_sum = lax.fori_loop(1, clus_n, far_in, fown[...])
    lanes = lax.broadcasted_iota(jnp.int32, (rows, rank_w), 1)
    far_fields = []
    for l in range(local_n):
        coeff = jnp.where(lanes < rank_ref[l], far_sum[l], 0.0).astype(BF16)
        swapped = turned(coeff.astype(F32), half).astype(BF16)
        far_fields.append(
            jnp.dot(coeff, cb[l, :rank_w], preferred_element_type=F32)
            + jnp.dot(swapped, cb[l, rank_w:], preferred_element_type=F32)
        )

    @pl.when(me_c > 0)
    def _():
        near_copy(1).wait_recv()

    @pl.when(me_c < clus_n - 1)
    def _():
        near_copy(0).wait_recv()

    for l in range(local_n):
        field = far_fields[l] + near_own[l] + nbr[0, l].astype(F32) + nbr[1, l].astype(F32)
        for p in range(2):
            out_ref[p, :, l * leaf : (l + 1) * leaf] = field[p * half : (p + 1) * half].astype(BF16)

    for copy in f_copies + n_copies:
        copy.wait_send()

    def far_sent(o, carry):
        far_copy(o).wait_send()
        return carry

    lax.fori_loop(1, clus_n, far_sent, 0)

    @pl.when(me_c > 0)
    def _():
        near_copy(0).wait_send()

    @pl.when(me_c < clus_n - 1)
    def _():
        near_copy(1).wait_send()


def body(clus_n, rhs_n, rhs_in, row_basis, col_basis, coupling, far_col, cluster_rank, near_block, near_col):
    _, half, width = rhs_in.shape
    local_n, _, rank_w, leaf = row_basis.shape
    far_n, near_n = coupling.shape[1], near_block.shape[1]
    rows = 2 * half
    rb = row_basis.reshape(local_n, 2 * rank_w, leaf)
    cb = col_basis.reshape(local_n, 2 * rank_w, leaf)
    nb = near_block.reshape(local_n, near_n, 2 * leaf, leaf)
    others, away = rhs_n - 1, clus_n - 1
    dma = pltpu.SemaphoreType.DMA
    smem = pl.BlockSpec(memory_space=pltpu.SMEM)
    vmem = pl.BlockSpec(memory_space=pltpu.VMEM)
    hbm = pl.BlockSpec(memory_space=pl.ANY)
    return pl.pallas_call(
        functools.partial(kernel, clus_n, rhs_n),
        out_shape=jax.ShapeDtypeStruct(rhs_in.shape, BF16),
        in_specs=[smem] * 3 + [vmem] + [hbm] * 4,
        out_specs=vmem,
        scratch_shapes=[
            pltpu.VMEM(rb.shape, BF16),
            pltpu.VMEM(coupling.shape, BF16),
            pltpu.VMEM(nb.shape, BF16),
            pltpu.VMEM(cb.shape, BF16),
            pltpu.VMEM((rows, width), BF16),
            pltpu.VMEM((others, rows, width), BF16),
            pltpu.VMEM((local_n * far_n, rhs_n * rows, rank_w), F32),
            pltpu.VMEM((rhs_n, clus_n, local_n, rows, rank_w), BF16),
            pltpu.VMEM((others, clus_n, local_n, rows, rank_w), BF16),
            pltpu.VMEM((local_n, rows, rank_w), F32),
            pltpu.VMEM((away, local_n, rows, rank_w), BF16),
            pltpu.VMEM((away, local_n, rows, rank_w), BF16),
            pltpu.VMEM((local_n * near_n, rhs_n * rows, leaf), F32),
            pltpu.VMEM((rhs_n, 3, local_n, rows, leaf), BF16),
            pltpu.VMEM((others, 3, local_n, rows, leaf), BF16),
            pltpu.VMEM((2, local_n, rows, leaf), BF16),
            pltpu.VMEM((2, local_n, rows, leaf), BF16),
            dma((4,)),
            dma((others,)),
            dma((others,)),
            dma((others,)),
            dma((others,)),
            dma((others,)),
            dma((others,)),
            dma((away,)),
            dma((away,)),
            dma((2,)),
            dma((2,)),
        ],
        compiler_params=pltpu.CompilerParams(
            collective_id=0, has_side_effects=True, vmem_limit_bytes=40 * 2**20
        ),
    )(cluster_rank, far_col, near_col, rhs_in, rb, coupling, nb, cb)


def solution(mesh):
    return jax.shard_map(
        functools.partial(body, mesh.shape["clus"], mesh.shape["rhs"]),
        mesh=mesh,
        in_specs=(
            P(None, "rhs", "clus"),
            P("clus", None, None, None),
            P("clus", None, None, None),
            P("clus", "rhs", None, None),
            P("clus", "rhs"),
            P("clus"),
            P("clus", "rhs", None, None, None),
            P("clus", "rhs"),
        ),
        out_specs=P(None, "rhs", "clus"),
        check_vma=False,
    )
```

```python
import functools

import jax
import jax.numpy as jnp
from jax import lax
from jax.experimental import pallas as pl
from jax.experimental.pallas import tpu as pltpu
from jax.sharding import PartitionSpec as P

MESH = pl.DeviceIdType.MESH
F32 = jnp.float32
BF16 = jnp.bfloat16


def turned(v, half):
    parts = []
    for start in range(0, v.shape[0], 2 * half):
        parts.append(-v[start + half : start + 2 * half])
        parts.append(v[start : start + half])
    return jnp.concatenate(parts, axis=0)


def kernel(
    clus_n, rhs_n,
    rank_ref, fcol_ref, ncol_ref, x_ref, rb_hbm, cp_hbm, nb_hbm, cb_hbm,
    out_ref,
    rb, cp, nb, cb, xs, xr, terms, fsend, frecv, fown, fbs, fbr, prods, nown, nsend, nrecv, nbs, nbr,
    load_sem, xs_sem, xr_sem, fs_sem, fr_sem, ns_sem, nr_sem, bs_sem, br_sem, ls_sem, lr_sem,
):
    me_c, me_r = lax.axis_index("clus"), lax.axis_index("rhs")
    half, leaf = x_ref.shape[1], nb.shape[3]
    rows = 2 * half
    local_n, near_n = nb.shape[0], nb.shape[1]
    far_n, rank_w = cp.shape[1], cp.shape[2]

    loads = [
        pltpu.make_async_copy(src, dst, load_sem.at[i])
        for i, (src, dst) in enumerate(((rb_hbm, rb), (cp_hbm, cp), (nb_hbm, nb), (cb_hbm, cb)))
    ]
    for load in loads:
        load.start()

    barrier = pltpu.get_barrier_semaphore()
    peers = [lax.rem(me_r + rhs_n - o, rhs_n) for o in range(rhs_n)]
    for o in range(1, rhs_n):
        pl.semaphore_signal(barrier, inc=1, device_id={"rhs": peers[o]}, device_id_type=MESH)

    def greet(o, carry):
        other = lax.rem(me_c + o, clus_n)
        pl.semaphore_signal(barrier, inc=1, device_id={"clus": other}, device_id_type=MESH)
        return carry

    lax.fori_loop(1, clus_n, greet, 0)
    xs[...] = jnp.concatenate([x_ref[0].astype(F32), x_ref[1].astype(F32)], axis=0).astype(BF16)

    @pl.when(me_c == 0)
    def _():
        nbr[0] = jnp.zeros_like(nbr[0])

    @pl.when(me_c == clus_n - 1)
    def _():
        nbr[1] = jnp.zeros_like(nbr[1])

    pl.semaphore_wait(barrier, rhs_n - 1 + clus_n - 1)

    def to_peer(src, dst, send, recv, o, forward=False):
        return pltpu.make_async_remote_copy(
            src_ref=src, dst_ref=dst.at[o - 1], send_sem=send.at[o - 1], recv_sem=recv.at[o - 1],
            device_id={"rhs": lax.rem(me_r + o, rhs_n) if forward else peers[o]}, device_id_type=MESH,
        )

    x_copies = [to_peer(xs, xr, xs_sem, xr_sem, o, forward=True) for o in range(1, rhs_n)]
    for copy in x_copies:
        copy.start()
    loads[0].wait()
    loads[1].wait()
    for copy in x_copies:
        copy.wait()

    fields = []
    for c in range(local_n):
        cols = slice(c * leaf, (c + 1) * leaf)
        plain = jnp.concatenate([xs[:, cols]] + [xr[o, :, cols] for o in range(rhs_n - 1)], axis=0)
        fields.append((plain, turned(plain.astype(F32), half).astype(BF16)))

    lanes = lax.broadcasted_iota(jnp.int32, (rhs_n * rows, rank_w), 1)
    last = (((1,), (1,)), ((), ()))
    for c in range(local_n):
        coeff = lax.dot_general(
            fields[c][0], rb[c, :rank_w], last, preferred_element_type=F32
        ) + lax.dot_general(fields[c][1], rb[c, rank_w:], last, preferred_element_type=F32)
        coeff = jnp.where(lanes < rank_ref[c], coeff, 0.0).astype(BF16)
        for f in range(far_n):
            coupled = jnp.dot(coeff, cp[c, f], preferred_element_type=F32)
            terms[c * far_n + f] = coupled[:, :rank_w] + turned(coupled[:, rank_w:], half)

    def spread(g, carry):
        for l in range(local_n):
            total = None
            for b in range(local_n * far_n):
                here = fcol_ref[b // far_n, b % far_n] == g * local_n + l
                part = terms[b] * jnp.where(here, 1.0, 0.0)
                total = part if total is None else total + part
            for o in range(rhs_n):
                fsend[o, g, l] = total[o * rows : (o + 1) * rows].astype(BF16)
        return carry

    lax.fori_loop(0, clus_n, spread, 0)
    f_copies = [to_peer(fsend.at[o], frecv, fs_sem, fr_sem, o) for o in range(1, rhs_n)]
    for copy in f_copies:
        copy.start()

    loads[2].wait()
    for c in range(local_n):
        both = jnp.concatenate(fields[c], axis=1)
        for n in range(near_n):
            prods[c * near_n + n] = jnp.dot(both, nb[c, n], preferred_element_type=F32)
    for d in range(3):
        for l in range(local_n):
            place = (d - 1) * local_n + l
            total = None
            for c in range(local_n):
                if abs(place - c) > 2:
                    continue
                for n in range(near_n):
                    here = ncol_ref[c, n] - me_c * local_n == place
                    part = prods[c * near_n + n] * jnp.where(here, 1.0, 0.0)
                    total = part if total is None else total + part
            if d == 1:
                nown[l] = total
            else:
                nbs[d // 2, l] = total.astype(BF16)

    def near_copy(side):
        other = me_c - 1 if side == 0 else me_c + 1
        return pltpu.make_async_remote_copy(
            src_ref=nbs.at[side], dst_ref=nbr.at[1 - side],
            send_sem=ls_sem.at[side], recv_sem=lr_sem.at[1 - side],
            device_id={"clus": other}, device_id_type=MESH,
        )

    @pl.when(me_c > 0)
    def _():
        near_copy(0).start()

    @pl.when(me_c < clus_n - 1)
    def _():
        near_copy(1).start()

    for copy in f_copies:
        copy.wait_recv()

    def far_here(g):
        total = fsend[0, g].astype(F32)
        for o in range(rhs_n - 1):
            total += frecv[o, g].astype(F32)
        return total

    def far_copy(o):
        return pltpu.make_async_remote_copy(
            src_ref=fbs.at[o - 1], dst_ref=fbr.at[o - 1],
            send_sem=bs_sem.at[o - 1], recv_sem=br_sem.at[o - 1],
            device_id={"clus": lax.rem(me_c + o, clus_n)}, device_id_type=MESH,
        )

    def far_out(o, carry):
        fbs[o - 1] = far_here(lax.rem(me_c + o, clus_n)).astype(BF16)
        far_copy(o).start()
        return carry

    lax.fori_loop(1, clus_n, far_out, 0)
    fown[...] = far_here(me_c)

    @pl.when(me_c > 0)
    def _():
        near_copy(1).wait_recv()

    @pl.when(me_c < clus_n - 1)
    def _():
        near_copy(0).wait_recv()

    near_own = []
    for l in range(local_n):
        total = nown[l] + nbr[0, l].astype(F32) + nbr[1, l].astype(F32)
        near_own.append(total[:rows])
        for o in range(1, rhs_n):
            nsend[o - 1, l] = total[o * rows : (o + 1) * rows].astype(BF16)
    n_copies = [to_peer(nsend.at[o - 1], nrecv, ns_sem, nr_sem, o) for o in range(1, rhs_n)]
    for copy in n_copies:
        copy.start()

    loads[3].wait()

    def far_in(o, total):
        far_copy(o).wait_recv()
        return total + fbr[o - 1].astype(F32)

    far_sum = lax.fori_loop(1, clus_n, far_in, fown[...])
    lanes = lax.broadcasted_iota(jnp.int32, (rows, rank_w), 1)
    far_fields = []
    for l in range(local_n):
        coeff = jnp.where(lanes < rank_ref[l], far_sum[l], 0.0).astype(BF16)
        swapped = turned(coeff.astype(F32), half).astype(BF16)
        far_fields.append(
            jnp.dot(coeff, cb[l, :rank_w], preferred_element_type=F32)
            + jnp.dot(swapped, cb[l, rank_w:], preferred_element_type=F32)
        )

    for copy in n_copies:
        copy.wait_recv()
    for l in range(local_n):
        field = far_fields[l] + near_own[l]
        for o in range(rhs_n - 1):
            field += nrecv[o, l].astype(F32)
        for p in range(2):
            out_ref[p, :, l * leaf : (l + 1) * leaf] = field[p * half : (p + 1) * half].astype(BF16)

    for copy in f_copies + n_copies:
        copy.wait_send()

    def far_sent(o, carry):
        far_copy(o).wait_send()
        return carry

    lax.fori_loop(1, clus_n, far_sent, 0)

    @pl.when(me_c > 0)
    def _():
        near_copy(0).wait_send()

    @pl.when(me_c < clus_n - 1)
    def _():
        near_copy(1).wait_send()


def body(clus_n, rhs_n, rhs_in, row_basis, col_basis, coupling, far_col, cluster_rank, near_block, near_col):
    _, half, width = rhs_in.shape
    local_n, _, rank_w, leaf = row_basis.shape
    far_n, near_n = coupling.shape[1], near_block.shape[1]
    rows = 2 * half
    rb = row_basis.reshape(local_n, 2 * rank_w, leaf)
    cb = col_basis.reshape(local_n, 2 * rank_w, leaf)
    nb = near_block.reshape(local_n, near_n, 2 * leaf, leaf)
    others, away = rhs_n - 1, clus_n - 1
    dma = pltpu.SemaphoreType.DMA
    smem = pl.BlockSpec(memory_space=pltpu.SMEM)
    vmem = pl.BlockSpec(memory_space=pltpu.VMEM)
    hbm = pl.BlockSpec(memory_space=pl.ANY)
    return pl.pallas_call(
        functools.partial(kernel, clus_n, rhs_n),
        out_shape=jax.ShapeDtypeStruct(rhs_in.shape, BF16),
        in_specs=[smem] * 3 + [vmem] + [hbm] * 4,
        out_specs=vmem,
        scratch_shapes=[
            pltpu.VMEM(rb.shape, BF16),
            pltpu.VMEM(coupling.shape, BF16),
            pltpu.VMEM(nb.shape, BF16),
            pltpu.VMEM(cb.shape, BF16),
            pltpu.VMEM((rows, width), BF16),
            pltpu.VMEM((others, rows, width), BF16),
            pltpu.VMEM((local_n * far_n, rhs_n * rows, rank_w), F32),
            pltpu.VMEM((rhs_n, clus_n, local_n, rows, rank_w), BF16),
            pltpu.VMEM((others, clus_n, local_n, rows, rank_w), BF16),
            pltpu.VMEM((local_n, rows, rank_w), F32),
            pltpu.VMEM((away, local_n, rows, rank_w), BF16),
            pltpu.VMEM((away, local_n, rows, rank_w), BF16),
            pltpu.VMEM((local_n * near_n, rhs_n * rows, leaf), F32),
            pltpu.VMEM((local_n, rhs_n * rows, leaf), F32),
            pltpu.VMEM((others, local_n, rows, leaf), BF16),
            pltpu.VMEM((others, local_n, rows, leaf), BF16),
            pltpu.VMEM((2, local_n, rhs_n * rows, leaf), BF16),
            pltpu.VMEM((2, local_n, rhs_n * rows, leaf), BF16),
            dma((4,)),
            dma((others,)),
            dma((others,)),
            dma((others,)),
            dma((others,)),
            dma((others,)),
            dma((others,)),
            dma((away,)),
            dma((away,)),
            dma((2,)),
            dma((2,)),
        ],
        compiler_params=pltpu.CompilerParams(
            collective_id=0, has_side_effects=True, vmem_limit_bytes=63 * 2**20
        ),
    )(cluster_rank, far_col, near_col, rhs_in, rb, coupling, nb, cb)


def solution(mesh):
    return jax.shard_map(
        functools.partial(body, mesh.shape["clus"], mesh.shape["rhs"]),
        mesh=mesh,
        in_specs=(
            P(None, "rhs", "clus"),
            P("clus", None, None, None),
            P("clus", None, None, None),
            P("clus", "rhs", None, None),
            P("clus", "rhs"),
            P("clus"),
            P("clus", "rhs", None, None, None),
            P("clus", "rhs"),
        ),
        out_specs=P(None, "rhs", "clus"),
        check_vma=False,
    )
```

```python
import functools
import math

import jax
import jax.numpy as jnp
from jax import lax
from jax.experimental import pallas as pl
from jax.experimental.pallas import tpu as pltpu
from jax.sharding import PartitionSpec as P

MESH = pl.DeviceIdType.MESH
F32 = jnp.float32
BF16 = jnp.bfloat16


def turned(v, half):
    parts = []
    for start in range(0, v.shape[0], 2 * half):
        parts.append(-v[start + half : start + 2 * half])
        parts.append(v[start : start + half])
    return jnp.concatenate(parts, axis=0)


def kernel(
    clus_n, rhs_n,
    rank_ref, fcol_ref, ncol_ref, x_ref, rb_hbm, cp_hbm, nb_hbm, cb_hbm,
    out_ref,
    rb, cp, nb, cb, xs, xr, terms, fsend, frecv, fbs, fbr, prods, nown, nsend, nrecv, nbs, nbr,
    load_sem, xs_sem, xr_sem, fs_sem, fr_sem, ns_sem, nr_sem, bs_sem, br_sem, ls_sem, lr_sem,
):
    me_c, me_r = lax.axis_index("clus"), lax.axis_index("rhs")
    half, leaf = x_ref.shape[1], nb.shape[3]
    rows = 2 * half
    local_n, near_n = nb.shape[0], nb.shape[1]
    far_n, rank_w = cp.shape[1], cp.shape[2]

    loads = [
        pltpu.make_async_copy(src, dst, load_sem.at[i])
        for i, (src, dst) in enumerate(((rb_hbm, rb), (cp_hbm, cp), (nb_hbm, nb), (cb_hbm, cb)))
    ]
    for load in loads:
        load.start()

    barrier = pltpu.get_barrier_semaphore()
    peers = [lax.rem(me_r + rhs_n - o, rhs_n) for o in range(rhs_n)]
    for o in range(1, rhs_n):
        pl.semaphore_signal(barrier, inc=1, device_id={"rhs": peers[o]}, device_id_type=MESH)

    def greet(o, carry):
        other = lax.rem(me_c + o, clus_n)
        pl.semaphore_signal(barrier, inc=1, device_id={"clus": other}, device_id_type=MESH)
        return carry

    lax.fori_loop(1, clus_n, greet, 0)
    xs[...] = jnp.concatenate([x_ref[0].astype(F32), x_ref[1].astype(F32)], axis=0).astype(BF16)

    @pl.when(me_c == 0)
    def _():
        nbr[0] = jnp.zeros_like(nbr[0])

    @pl.when(me_c == clus_n - 1)
    def _():
        nbr[1] = jnp.zeros_like(nbr[1])

    pl.semaphore_wait(barrier, rhs_n - 1 + clus_n - 1)

    def to_peer(src, dst, send, recv, o, forward=False):
        return pltpu.make_async_remote_copy(
            src_ref=src, dst_ref=dst.at[o - 1], send_sem=send.at[o - 1], recv_sem=recv.at[o - 1],
            device_id={"rhs": lax.rem(me_r + o, rhs_n) if forward else peers[o]}, device_id_type=MESH,
        )

    x_copies = [to_peer(xs, xr, xs_sem, xr_sem, o, forward=True) for o in range(1, rhs_n)]
    for copy in x_copies:
        copy.start()
    loads[0].wait()
    loads[1].wait()
    for copy in x_copies:
        copy.wait()

    fields = []
    for c in range(local_n):
        cols = slice(c * leaf, (c + 1) * leaf)
        plain = jnp.concatenate([xs[:, cols]] + [xr[o, :, cols] for o in range(rhs_n - 1)], axis=0)
        fields.append((plain, turned(plain.astype(F32), half).astype(BF16)))

    lanes = lax.broadcasted_iota(jnp.int32, (rhs_n * rows, rank_w), 1)
    last = (((1,), (1,)), ((), ()))
    for c in range(local_n):
        coeff = lax.dot_general(
            fields[c][0], rb[c, :rank_w], last, preferred_element_type=F32
        ) + lax.dot_general(fields[c][1], rb[c, rank_w:], last, preferred_element_type=F32)
        coeff = jnp.where(lanes < rank_ref[c], coeff, 0.0).astype(BF16)
        for f in range(far_n):
            coupled = jnp.dot(coeff, cp[c, f], preferred_element_type=F32)
            terms[c * far_n + f] = coupled[:, :rank_w] + turned(coupled[:, rank_w:], half)

    packs = fsend.shape[1]
    pack_n = fsend.shape[3] // rank_w

    def far_part(o, h):
        return pltpu.make_async_remote_copy(
            src_ref=fsend.at[o, h], dst_ref=frecv.at[o - 1, h],
            send_sem=fs_sem.at[o - 1, h], recv_sem=fr_sem.at[o - 1, h],
            device_id={"rhs": peers[o]}, device_id_type=MESH,
        )

    def spread(h, carry):
        totals = []
        for j in range(pack_n):
            total = None
            for b in range(local_n * far_n):
                here = fcol_ref[b // far_n, b % far_n] == h * pack_n + j
                part = terms[b] * jnp.where(here, 1.0, 0.0)
                total = part if total is None else total + part
            totals.append(total)
        packed = jnp.concatenate(totals, axis=1)
        for o in range(rhs_n):
            fsend[o, h] = packed[o * rows : (o + 1) * rows].astype(BF16)
            if o:
                far_part(o, h).start()
        return carry

    lax.fori_loop(0, packs, spread, 0)

    loads[2].wait()
    for c in range(local_n):
        both = jnp.concatenate(fields[c], axis=1)
        for n in range(near_n):
            prods[c * near_n + n] = jnp.dot(both, nb[c, n], preferred_element_type=F32)
    for d in range(3):
        for l in range(local_n):
            place = (d - 1) * local_n + l
            total = None
            for c in range(local_n):
                if abs(place - c) > 2:
                    continue
                for n in range(near_n):
                    here = ncol_ref[c, n] - me_c * local_n == place
                    part = prods[c * near_n + n] * jnp.where(here, 1.0, 0.0)
                    total = part if total is None else total + part
            if d == 1:
                nown[l] = total
            else:
                nbs[d // 2, l] = total.astype(BF16)

    def near_copy(side):
        other = me_c - 1 if side == 0 else me_c + 1
        return pltpu.make_async_remote_copy(
            src_ref=nbs.at[side], dst_ref=nbr.at[1 - side],
            send_sem=ls_sem.at[side], recv_sem=lr_sem.at[1 - side],
            device_id={"clus": other}, device_id_type=MESH,
        )

    @pl.when(me_c > 0)
    def _():
        near_copy(0).start()

    @pl.when(me_c < clus_n - 1)
    def _():
        near_copy(1).start()

    def far_copy(g, slot):
        return pltpu.make_async_remote_copy(
            src_ref=fbs.at[g], dst_ref=fbr.at[slot],
            send_sem=bs_sem.at[g], recv_sem=br_sem.at[slot],
            device_id={"clus": g}, device_id_type=MESH,
        )

    def far_out(h, carry):
        total = fsend[0, h].astype(F32)
        for o in range(1, rhs_n):
            far_part(o, h).wait_recv()
            total += frecv[o - 1, h].astype(F32)
        for i in range(pack_n // local_n):
            g = h * (pack_n // local_n) + i
            for l in range(local_n):
                j = i * local_n + l
                fbs[g, l] = total[:, j * rank_w : (j + 1) * rank_w].astype(BF16)

            @pl.when(g != me_c)
            def _():
                far_copy(g, me_c).start()

        return carry

    lax.fori_loop(0, packs, far_out, 0)

    @pl.when(me_c > 0)
    def _():
        near_copy(1).wait_recv()

    @pl.when(me_c < clus_n - 1)
    def _():
        near_copy(0).wait_recv()

    near_own = []
    for l in range(local_n):
        total = nown[l] + nbr[0, l].astype(F32) + nbr[1, l].astype(F32)
        near_own.append(total[:rows])
        for o in range(1, rhs_n):
            nsend[o - 1, l] = total[o * rows : (o + 1) * rows].astype(BF16)
    n_copies = [to_peer(nsend.at[o - 1], nrecv, ns_sem, nr_sem, o) for o in range(1, rhs_n)]
    for copy in n_copies:
        copy.start()

    loads[3].wait()

    def far_in(o, total):
        slot = lax.rem(me_c + o, clus_n)
        far_copy(slot, slot).wait_recv()
        return total + fbr[slot].astype(F32)

    far_sum = lax.fori_loop(1, clus_n, far_in, fbs[me_c].astype(F32))
    lanes = lax.broadcasted_iota(jnp.int32, (rows, rank_w), 1)
    far_fields = []
    for l in range(local_n):
        coeff = jnp.where(lanes < rank_ref[l], far_sum[l], 0.0).astype(BF16)
        swapped = turned(coeff.astype(F32), half).astype(BF16)
        far_fields.append(
            jnp.dot(coeff, cb[l, :rank_w], preferred_element_type=F32)
            + jnp.dot(swapped, cb[l, rank_w:], preferred_element_type=F32)
        )

    for copy in n_copies:
        copy.wait_recv()
    for l in range(local_n):
        field = far_fields[l] + near_own[l]
        for o in range(rhs_n - 1):
            field += nrecv[o, l].astype(F32)
        for p in range(2):
            out_ref[p, :, l * leaf : (l + 1) * leaf] = field[p * half : (p + 1) * half].astype(BF16)

    for copy in n_copies:
        copy.wait_send()

    def parts_sent(h, carry):
        for o in range(1, rhs_n):
            far_part(o, h).wait_send()
        return carry

    lax.fori_loop(0, packs, parts_sent, 0)

    def far_sent(o, carry):
        slot = lax.rem(me_c + o, clus_n)
        far_copy(slot, slot).wait_send()
        return carry

    lax.fori_loop(1, clus_n, far_sent, 0)

    @pl.when(me_c > 0)
    def _():
        near_copy(0).wait_send()

    @pl.when(me_c < clus_n - 1)
    def _():
        near_copy(1).wait_send()


def body(clus_n, rhs_n, rhs_in, row_basis, col_basis, coupling, far_col, cluster_rank, near_block, near_col):
    _, half, width = rhs_in.shape
    local_n, _, rank_w, leaf = row_basis.shape
    far_n, near_n = coupling.shape[1], near_block.shape[1]
    rows = 2 * half
    rb = row_basis.reshape(local_n, 2 * rank_w, leaf)
    cb = col_basis.reshape(local_n, 2 * rank_w, leaf)
    nb = near_block.reshape(local_n, near_n, 2 * leaf, leaf)
    others = rhs_n - 1
    pack_n = math.lcm(128 // math.gcd(rank_w, 128), local_n)
    packs = clus_n * local_n // pack_n
    dma = pltpu.SemaphoreType.DMA
    smem = pl.BlockSpec(memory_space=pltpu.SMEM)
    vmem = pl.BlockSpec(memory_space=pltpu.VMEM)
    hbm = pl.BlockSpec(memory_space=pl.ANY)
    return pl.pallas_call(
        functools.partial(kernel, clus_n, rhs_n),
        out_shape=jax.ShapeDtypeStruct(rhs_in.shape, BF16),
        in_specs=[smem] * 3 + [vmem] + [hbm] * 4,
        out_specs=vmem,
        scratch_shapes=[
            pltpu.VMEM(rb.shape, BF16),
            pltpu.VMEM(coupling.shape, BF16),
            pltpu.VMEM(nb.shape, BF16),
            pltpu.VMEM(cb.shape, BF16),
            pltpu.VMEM((rows, width), BF16),
            pltpu.VMEM((others, rows, width), BF16),
            pltpu.VMEM((local_n * far_n, rhs_n * rows, rank_w), F32),
            pltpu.VMEM((rhs_n, packs, rows, pack_n * rank_w), BF16),
            pltpu.VMEM((others, packs, rows, pack_n * rank_w), BF16),
            pltpu.VMEM((clus_n, local_n, rows, rank_w), BF16),
            pltpu.VMEM((clus_n, local_n, rows, rank_w), BF16),
            pltpu.VMEM((local_n * near_n, rhs_n * rows, leaf), F32),
            pltpu.VMEM((local_n, rhs_n * rows, leaf), F32),
            pltpu.VMEM((others, local_n, rows, leaf), BF16),
            pltpu.VMEM((others, local_n, rows, leaf), BF16),
            pltpu.VMEM((2, local_n, rhs_n * rows, leaf), BF16),
            pltpu.VMEM((2, local_n, rhs_n * rows, leaf), BF16),
            dma((4,)),
            dma((others,)),
            dma((others,)),
            dma((others, packs)),
            dma((others, packs)),
            dma((others,)),
            dma((others,)),
            dma((clus_n,)),
            dma((clus_n,)),
            dma((2,)),
            dma((2,)),
        ],
        compiler_params=pltpu.CompilerParams(
            collective_id=0, has_side_effects=True, vmem_limit_bytes=63 * 2**20
        ),
    )(cluster_rank, far_col, near_col, rhs_in, rb, coupling, nb, cb)


def solution(mesh):
    return jax.shard_map(
        functools.partial(body, mesh.shape["clus"], mesh.shape["rhs"]),
        mesh=mesh,
        in_specs=(
            P(None, "rhs", "clus"),
            P("clus", None, None, None),
            P("clus", None, None, None),
            P("clus", "rhs", None, None),
            P("clus", "rhs"),
            P("clus"),
            P("clus", "rhs", None, None, None),
            P("clus", "rhs"),
        ),
        out_specs=P(None, "rhs", "clus"),
        check_vma=False,
    )
```

```python
import functools
import math

import jax
import jax.numpy as jnp
from jax import lax
from jax.experimental import pallas as pl
from jax.experimental.pallas import tpu as pltpu
from jax.sharding import PartitionSpec as P

MESH = pl.DeviceIdType.MESH
F32 = jnp.float32
BF16 = jnp.bfloat16


def turned(v, half):
    parts = []
    for start in range(0, v.shape[0], 2 * half):
        parts.append(-v[start + half : start + 2 * half])
        parts.append(v[start : start + half])
    return jnp.concatenate(parts, axis=0)


def kernel(
    clus_n, rhs_n,
    rank_ref, fcol_ref, ncol_ref, x_ref, rb_hbm, cp_hbm, nb_hbm, cb_hbm,
    out_ref,
    rb, cp, nb, cb, xs, xr, terms, fsend, frecv, fbs, fbr, prods, nown, nsend, nrecv, nbs, nbr,
    load_sem, xs_sem, xr_sem, fs_sem, fr_sem, ns_sem, nr_sem, bs_sem, br_sem, ls_sem, lr_sem,
):
    me_c, me_r = lax.axis_index("clus"), lax.axis_index("rhs")
    half, leaf = x_ref.shape[1], nb.shape[3]
    rows = 2 * half
    local_n, near_n = nb.shape[0], nb.shape[1]
    far_n, rank_w = cp.shape[1], cp.shape[2]

    loads = [
        pltpu.make_async_copy(src, dst, load_sem.at[i])
        for i, (src, dst) in enumerate(((rb_hbm, rb), (cp_hbm, cp), (nb_hbm, nb), (cb_hbm, cb)))
    ]
    for load in loads:
        load.start()

    barrier = pltpu.get_barrier_semaphore()
    peers = [lax.rem(me_r + rhs_n - o, rhs_n) for o in range(rhs_n)]
    for o in range(1, rhs_n):
        pl.semaphore_signal(barrier, inc=1, device_id={"rhs": peers[o]}, device_id_type=MESH)

    def greet(o, carry):
        other = lax.rem(me_c + o, clus_n)
        pl.semaphore_signal(barrier, inc=1, device_id={"clus": other}, device_id_type=MESH)
        return carry

    lax.fori_loop(1, clus_n, greet, 0)
    xs[...] = jnp.concatenate([x_ref[0].astype(F32), x_ref[1].astype(F32)], axis=0).astype(BF16)

    @pl.when(me_c == 0)
    def _():
        nbr[0] = jnp.zeros_like(nbr[0])

    @pl.when(me_c == clus_n - 1)
    def _():
        nbr[1] = jnp.zeros_like(nbr[1])

    pl.semaphore_wait(barrier, rhs_n - 1 + clus_n - 1)

    def to_peer(src, dst, send, recv, o, forward=False):
        return pltpu.make_async_remote_copy(
            src_ref=src, dst_ref=dst.at[o - 1], send_sem=send.at[o - 1], recv_sem=recv.at[o - 1],
            device_id={"rhs": lax.rem(me_r + o, rhs_n) if forward else peers[o]}, device_id_type=MESH,
        )

    x_copies = [to_peer(xs, xr, xs_sem, xr_sem, o, forward=True) for o in range(1, rhs_n)]
    for copy in x_copies:
        copy.start()
    loads[0].wait()
    loads[1].wait()
    for copy in x_copies:
        copy.wait()

    fields = []
    for c in range(local_n):
        cols = slice(c * leaf, (c + 1) * leaf)
        plain = jnp.concatenate([xs[:, cols]] + [xr[o, :, cols] for o in range(rhs_n - 1)], axis=0)
        fields.append((plain, turned(plain.astype(F32), half).astype(BF16)))

    lanes = lax.broadcasted_iota(jnp.int32, (rhs_n * rows, rank_w), 1)
    last = (((1,), (1,)), ((), ()))
    for c in range(local_n):
        coeff = lax.dot_general(
            fields[c][0], rb[c, :rank_w], last, preferred_element_type=F32
        ) + lax.dot_general(fields[c][1], rb[c, rank_w:], last, preferred_element_type=F32)
        coeff = jnp.where(lanes < rank_ref[c], coeff, 0.0).astype(BF16)
        for f in range(far_n):
            coupled = jnp.dot(coeff, cp[c, f], preferred_element_type=F32)
            terms[c * far_n + f] = coupled[:, :rank_w] + turned(coupled[:, rank_w:], half)

    packs = fsend.shape[1]
    pack_n = fsend.shape[3] // rank_w

    def far_part(o, h):
        return pltpu.make_async_remote_copy(
            src_ref=fsend.at[o, h], dst_ref=frecv.at[o - 1, h],
            send_sem=fs_sem.at[o - 1, h], recv_sem=fr_sem.at[o - 1, h],
            device_id={"rhs": peers[o]}, device_id_type=MESH,
        )

    def spread(h, carry):
        totals = []
        for j in range(pack_n):
            total = None
            for b in range(local_n * far_n):
                here = fcol_ref[b // far_n, b % far_n] == h * pack_n + j
                part = terms[b] * jnp.where(here, 1.0, 0.0)
                total = part if total is None else total + part
            totals.append(total)
        packed = jnp.concatenate(totals, axis=1)
        for o in range(rhs_n):
            fsend[o, h] = packed[o * rows : (o + 1) * rows].astype(BF16)
            if o:
                far_part(o, h).start()
        return carry

    lax.fori_loop(0, packs, spread, 0)

    loads[2].wait()
    for c in range(local_n):
        both = jnp.concatenate(fields[c], axis=1)
        for n in range(near_n):
            prods[c * near_n + n] = jnp.dot(both, nb[c, n], preferred_element_type=F32)
    def near_copy(side):
        other = me_c - 1 if side == 0 else me_c + 1
        return pltpu.make_async_remote_copy(
            src_ref=nbs.at[side], dst_ref=nbr.at[1 - side],
            send_sem=ls_sem.at[side], recv_sem=lr_sem.at[1 - side],
            device_id={"clus": other}, device_id_type=MESH,
        )

    def band(d):
        for l in range(local_n):
            place = (d - 1) * local_n + l
            total = None
            for c in range(local_n):
                if abs(place - c) > 2:
                    continue
                for n in range(near_n):
                    here = ncol_ref[c, n] - me_c * local_n == place
                    part = prods[c * near_n + n] * jnp.where(here, 1.0, 0.0)
                    total = part if total is None else total + part
            if d == 1:
                nown[l] = total
            else:
                nbs[d // 2, l] = total.astype(BF16)

    band(0)

    @pl.when(me_c > 0)
    def _():
        near_copy(0).start()

    band(2)

    @pl.when(me_c < clus_n - 1)
    def _():
        near_copy(1).start()

    band(1)

    def far_copy(g, slot):
        return pltpu.make_async_remote_copy(
            src_ref=fbs.at[g], dst_ref=fbr.at[slot],
            send_sem=bs_sem.at[g], recv_sem=br_sem.at[slot],
            device_id={"clus": g}, device_id_type=MESH,
        )

    def far_out(h, carry):
        total = fsend[0, h].astype(F32)
        for o in range(1, rhs_n):
            far_part(o, h).wait_recv()
            total += frecv[o - 1, h].astype(F32)
        for i in range(pack_n // local_n):
            g = h * (pack_n // local_n) + i
            for l in range(local_n):
                j = i * local_n + l
                fbs[g, l] = total[:, j * rank_w : (j + 1) * rank_w].astype(BF16)

            @pl.when(g != me_c)
            def _():
                far_copy(g, me_c).start()

        return carry

    lax.fori_loop(0, packs, far_out, 0)

    @pl.when(me_c > 0)
    def _():
        near_copy(1).wait_recv()

    @pl.when(me_c < clus_n - 1)
    def _():
        near_copy(0).wait_recv()

    near_own = []
    for l in range(local_n):
        total = nown[l] + nbr[0, l].astype(F32) + nbr[1, l].astype(F32)
        near_own.append(total[:rows])
        for o in range(1, rhs_n):
            nsend[o - 1, l] = total[o * rows : (o + 1) * rows].astype(BF16)
    n_copies = [to_peer(nsend.at[o - 1], nrecv, ns_sem, nr_sem, o) for o in range(1, rhs_n)]
    for copy in n_copies:
        copy.start()

    loads[3].wait()

    def far_in(o, total):
        slot = lax.rem(me_c + o, clus_n)
        far_copy(slot, slot).wait_recv()
        return total + fbr[slot].astype(F32)

    far_sum = lax.fori_loop(1, clus_n, far_in, fbs[me_c].astype(F32))
    lanes = lax.broadcasted_iota(jnp.int32, (rows, rank_w), 1)
    far_fields = []
    for l in range(local_n):
        coeff = jnp.where(lanes < rank_ref[l], far_sum[l], 0.0).astype(BF16)
        swapped = turned(coeff.astype(F32), half).astype(BF16)
        far_fields.append(
            jnp.dot(coeff, cb[l, :rank_w], preferred_element_type=F32)
            + jnp.dot(swapped, cb[l, rank_w:], preferred_element_type=F32)
        )

    for copy in n_copies:
        copy.wait_recv()
    for l in range(local_n):
        field = far_fields[l] + near_own[l]
        for o in range(rhs_n - 1):
            field += nrecv[o, l].astype(F32)
        for p in range(2):
            out_ref[p, :, l * leaf : (l + 1) * leaf] = field[p * half : (p + 1) * half].astype(BF16)

    for copy in n_copies:
        copy.wait_send()

    def parts_sent(h, carry):
        for o in range(1, rhs_n):
            far_part(o, h).wait_send()
        return carry

    lax.fori_loop(0, packs, parts_sent, 0)

    def far_sent(o, carry):
        slot = lax.rem(me_c + o, clus_n)
        far_copy(slot, slot).wait_send()
        return carry

    lax.fori_loop(1, clus_n, far_sent, 0)

    @pl.when(me_c > 0)
    def _():
        near_copy(0).wait_send()

    @pl.when(me_c < clus_n - 1)
    def _():
        near_copy(1).wait_send()


def body(clus_n, rhs_n, rhs_in, row_basis, col_basis, coupling, far_col, cluster_rank, near_block, near_col):
    _, half, width = rhs_in.shape
    local_n, _, rank_w, leaf = row_basis.shape
    far_n, near_n = coupling.shape[1], near_block.shape[1]
    rows = 2 * half
    rb = row_basis.reshape(local_n, 2 * rank_w, leaf)
    cb = col_basis.reshape(local_n, 2 * rank_w, leaf)
    nb = near_block.reshape(local_n, near_n, 2 * leaf, leaf)
    others = rhs_n - 1
    pack_n = math.lcm(128 // math.gcd(rank_w, 128), local_n)
    packs = clus_n * local_n // pack_n
    dma = pltpu.SemaphoreType.DMA
    smem = pl.BlockSpec(memory_space=pltpu.SMEM)
    vmem = pl.BlockSpec(memory_space=pltpu.VMEM)
    hbm = pl.BlockSpec(memory_space=pl.ANY)
    return pl.pallas_call(
        functools.partial(kernel, clus_n, rhs_n),
        out_shape=jax.ShapeDtypeStruct(rhs_in.shape, BF16),
        in_specs=[smem] * 3 + [vmem] + [hbm] * 4,
        out_specs=vmem,
        scratch_shapes=[
            pltpu.VMEM(rb.shape, BF16),
            pltpu.VMEM(coupling.shape, BF16),
            pltpu.VMEM(nb.shape, BF16),
            pltpu.VMEM(cb.shape, BF16),
            pltpu.VMEM((rows, width), BF16),
            pltpu.VMEM((others, rows, width), BF16),
            pltpu.VMEM((local_n * far_n, rhs_n * rows, rank_w), F32),
            pltpu.VMEM((rhs_n, packs, rows, pack_n * rank_w), BF16),
            pltpu.VMEM((others, packs, rows, pack_n * rank_w), BF16),
            pltpu.VMEM((clus_n, local_n, rows, rank_w), BF16),
            pltpu.VMEM((clus_n, local_n, rows, rank_w), BF16),
            pltpu.VMEM((local_n * near_n, rhs_n * rows, leaf), F32),
            pltpu.VMEM((local_n, rhs_n * rows, leaf), F32),
            pltpu.VMEM((others, local_n, rows, leaf), BF16),
            pltpu.VMEM((others, local_n, rows, leaf), BF16),
            pltpu.VMEM((2, local_n, rhs_n * rows, leaf), BF16),
            pltpu.VMEM((2, local_n, rhs_n * rows, leaf), BF16),
            dma((4,)),
            dma((others,)),
            dma((others,)),
            dma((others, packs)),
            dma((others, packs)),
            dma((others,)),
            dma((others,)),
            dma((clus_n,)),
            dma((clus_n,)),
            dma((2,)),
            dma((2,)),
        ],
        compiler_params=pltpu.CompilerParams(
            collective_id=0, has_side_effects=True, vmem_limit_bytes=63 * 2**20
        ),
    )(cluster_rank, far_col, near_col, rhs_in, rb, coupling, nb, cb)


def solution(mesh):
    return jax.shard_map(
        functools.partial(body, mesh.shape["clus"], mesh.shape["rhs"]),
        mesh=mesh,
        in_specs=(
            P(None, "rhs", "clus"),
            P("clus", None, None, None),
            P("clus", None, None, None),
            P("clus", "rhs", None, None),
            P("clus", "rhs"),
            P("clus"),
            P("clus", "rhs", None, None, None),
            P("clus", "rhs"),
        ),
        out_specs=P(None, "rhs", "clus"),
        check_vma=False,
    )
```
